256 devices in a mesh: shard: 32 (over y, z), worker: 8 (over x, core).
Axes of the slice: x: 4, y: 4, z: 8, core: 2. Of those that a mesh axis runs over, the one named last changes fastest.
Arguments:
- grads: bfloat16 [32, 1024, 1024], P(None, 'shard'), may hold values from -0.29882812 to 0.29882812
- owners: int32 [32, 1], replicated, may hold values from 0 to 7; in each aligned block of 32 rows (0 to 31, 32 to 63, ...) at most 6 rows name the same one
- left: float32 [8, 6, 1024, 1024], P('worker', None, 'shard'), as said below
- right: float32 [8, 6, 1024, 1024], P('worker', None, 'shard'), as said below
- left_root: float32 [8, 6, 1024, 1024], P('worker', None, 'shard'), as said below
- right_root: float32 [8, 6, 1024, 1024], P('worker', None, 'shard'), as said below
Outputs:
- new_left: float32 [8, 6, 1024, 1024], P('worker', None, 'shard')
- new_right: float32 [8, 6, 1024, 1024], P('worker', None, 'shard')
- precond: bfloat16 [32, 1024, 1024], P(None, 'shard')
The draws below stay inside these ranges and needn't reach their ends.
Inputs may be any that keep to these rules, and one draw needn't show every extreme that they name: `owners`: no worker owns more than 6 blocks, and some worker owns exactly 6. `left`: each matrix is symmetric with a positive diagonal. `right`: each matrix is symmetric with a positive diagonal. `left_root`: each matrix is symmetric with a positive diagonal. `right_root`: each matrix is symmetric with a positive diagonal.
All inputs are finite; a program needn't handle non-finite values.
Results may differ from the reference program's by a relative error of at most 0.0049.
Values may be sent and summed in bfloat16 or wider, within the bound.
No kernel may reach another device: no remote copies, remote signals or barrier semaphores. Data moves between devices by JAX's collectives and lax.ppermute only.
A program may use at most 128 MiB of HBM per device.

```python
import math
import jax
import jax.numpy as jnp
import numpy as np
from jax import lax

BS = 1024
NB = 32
CAP = 6
N_WORKER = 8


def symmetric_from(key, offdiag, lower, upper):
    shape = (N_WORKER, CAP, BS, BS)
    diag_vals = jax.random.uniform(key, shape[:3], jnp.float32, lower, upper)
    sym = (offdiag + jnp.swapaxes(offdiag, 2, 3)) * 0.7071
    eye = (lax.broadcasted_iota(jnp.int32, (BS, BS), 0) == lax.broadcasted_iota(jnp.int32, (BS, BS), 1)).astype(jnp.float32)
    return sym * (1.0 - eye) + eye * diag_vals[..., None]


def offdiag_draw(key, scale):
    shape = (N_WORKER, CAP, BS, BS)
    return jax.random.normal(key, shape, jnp.float32) * scale


def draw_left(key, part):
    key = jax.random.fold_in(key, 11)
    first, second = jax.random.split(key)
    return symmetric_from(second, offdiag_draw(first, 1.0 / math.sqrt(BS)), 1.0, 4.0)


def draw_right(key, part):
    key = jax.random.fold_in(key, 23)
    first, second = jax.random.split(key)
    return symmetric_from(second, offdiag_draw(first, 1.0 / math.sqrt(BS)), 1.0, 4.0)


def draw_left_root(key, part):
    key = jax.random.fold_in(key, 37)
    first, second = jax.random.split(key)
    return symmetric_from(second, offdiag_draw(first, 0.5 / math.sqrt(BS)), 0.5, 1.5)


def draw_right_root(key, part):
    key = jax.random.fold_in(key, 41)
    first, second = jax.random.split(key)
    return symmetric_from(second, offdiag_draw(first, 0.5 / math.sqrt(BS)), 0.5, 1.5)


def shard_levels(stream_key, shape, shards, low, largest):
    factor_of = 1.0
    for dim, shards_of in shards:
        draws = jax.random.uniform(jax.random.fold_in(jax.random.fold_in(stream_key, 6), dim), (shards_of,), jnp.float32, low / len(shards), largest / len(shards))
        factor_of = factor_of * jnp.repeat(jnp.exp(draws), shape[dim] // shards_of).reshape((-1,) + (1,) * (len(shape) - 1 - dim))
    return factor_of


def routed_block(stream_key, own, number, rows, number_of, top, reach, skew):
    sequence = jax.random.permutation(stream_key, number_of)
    packed, ordinary = shares(number_of, rows * top, reach, skew, True), shares(number_of, rows * top, reach, skew, False)
    places = jnp.arange(number_of)

    def named(sizes, offset_by):
        used = int((sizes > 0).sum())
        fixed = max(1, used // 4)
        passed = fixed + (places - fixed + offset_by * (used - fixed)) % max(1, number_of - fixed)
        return jnp.zeros((number_of,), jnp.int32).at[sequence[jnp.where(places < fixed, places, passed)]].set(jnp.asarray(sizes, jnp.int32))

    sizes = jnp.where(number % 4 == 0, named(packed, number // 4), named(ordinary, number - number // 4 - 1))
    mixed = jax.random.permutation(jax.random.fold_in(own, 3), number_of)
    source_of, sink = mixed[0:number_of // 2 * 2:2], mixed[1:number_of // 2 * 2:2]
    room = jnp.minimum(sizes[source_of] - 1, reach - sizes[sink]) // 2
    room = jnp.where((source_of == sequence[0]) | (sink == sequence[0]) | (sizes[sink] == 0), 0, jnp.maximum(room, 0))
    passed = jax.random.randint(jax.random.fold_in(own, 4), (number_of // 2,), 0, 1 << 20) % (room + 1)
    sizes = sizes.at[source_of].add(-passed).at[sink].add(passed)
    items = jnp.searchsorted(jnp.cumsum(sizes), jnp.arange(rows * top), side="right").astype(jnp.int32)
    table = items.reshape(top, rows).T
    table = table[jax.random.permutation(jax.random.fold_in(own, 1), rows)]
    offset_by = jax.random.randint(jax.random.fold_in(own, 2), (rows, 1), 0, top)
    return jnp.take_along_axis(table, (jnp.arange(top)[None, :] + offset_by) % top, axis=1)


def shares(number_of, total, most, skew, full):
    portions = [(1 << 20) // math.isqrt(grade ** skew) + 1 for grade in range(1, number_of + 1)]
    largest = most if full else min(most, max(-(-total // number_of), total * portions[0] // sum(portions)))
    least = 1 if total - largest >= number_of - 1 else 0
    holding, spare = [largest] + [least] * (number_of - 1), total - largest - least * (number_of - 1)
    while spare > 0:
        movable = [i for i in range(1, number_of) if holding[i] < largest] or [i for i in range(1, number_of) if holding[i] < most]
        mass, budget = sum([portions[i] for i in movable]), spare
        for i in movable:
            addition = min(most - holding[i], max(1, budget * portions[i] // mass), spare)
            holding[i] = holding[i] + addition
            spare = spare - addition
    return np.array(holding)


def scatter_about(rng, dims, deviation, limit, shards=(), kind=jnp.bfloat16):
    array = jax.random.normal(rng, dims, jnp.float32) * deviation
    if len(shards) > 0:
        array = shard_levels(rng, dims, shards, -0.22, 0.18) * array
    return jnp.clip(array, min=-limit, max=limit).astype(kind)


def setup_inputs(seed: int = 0) -> dict:
    streams_of = jax.random.split(jax.random.key(seed), 7)
    grads = scatter_about(streams_of[0], (NB, BS, BS), 0.05, 0.29882812, ((1, 32),))
    owners_keys = jax.random.split(jax.random.fold_in(streams_of[1], 1), NB // NB)
    owners_turns = jax.random.permutation(jax.random.fold_in(streams_of[1], 3), NB // NB)
    owners = jax.vmap(lambda own, number: routed_block(jax.random.fold_in(streams_of[1], 2), own, number, NB, N_WORKER, 1, CAP, 2))(owners_keys, owners_turns).reshape((NB, 1))
    left = draw_left(jax.random.fold_in(streams_of[6], 71), 0)
    right = draw_right(jax.random.fold_in(streams_of[6], 71), 0)
    left_root = draw_left_root(jax.random.fold_in(streams_of[6], 71), 0)
    right_root = draw_right_root(jax.random.fold_in(streams_of[6], 71), 0)
    return dict(grads=grads, owners=owners, left=left, right=right, left_root=left_root, right_root=right_root)


decay_rate = 0.9


def slot_table(owner):
    count = owner.shape[0]
    earlier = lax.broadcasted_iota(jnp.int32, (count, count), 1) < lax.broadcasted_iota(jnp.int32, (count, count), 0)
    same = owner[:, None] == owner[None, :]
    return jnp.sum((same & earlier).astype(jnp.int32), axis=1).astype(jnp.int32)


def reference(grads, owners, left, right, left_root, right_root):
    owner = owners[:, 0].astype(jnp.int32)
    slot = slot_table(owner)
    flat = (owner * CAP + slot).astype(jnp.int32)
    left_flat = left.reshape(N_WORKER * CAP, BS, BS)
    right_flat = right.reshape(N_WORKER * CAP, BS, BS)
    lroot_flat = left_root.reshape(N_WORKER * CAP, BS, BS)
    rroot_flat = right_root.reshape(N_WORKER * CAP, BS, BS)

    def one_block(index):
        block = grads[index]
        where = flat[index]
        gram_left = jnp.dot(block, block.T, preferred_element_type=jnp.float32)
        gram_right = jnp.dot(block.T, block, preferred_element_type=jnp.float32)
        upd_left = decay_rate * left_flat[where] + (1.0 - decay_rate) * gram_left
        upd_right = decay_rate * right_flat[where] + (1.0 - decay_rate) * gram_right
        image_t = jnp.dot(rroot_flat[where], block.astype(jnp.float32).T, precision=lax.Precision.HIGHEST).astype(jnp.bfloat16)
        result = jnp.dot(lroot_flat[where], image_t.astype(jnp.float32).T, precision=lax.Precision.HIGHEST).astype(jnp.bfloat16)
        return upd_left, upd_right, result

    upd_left, upd_right, precond = lax.map(one_block, jnp.arange(NB, dtype=jnp.int32))
    new_left = left_flat.at[flat].set(upd_left).reshape(left.shape)
    new_right = right_flat.at[flat].set(upd_right).reshape(right.shape)
    return new_left, new_right, precond
```

```python
import jax
import jax.numpy as jnp
from jax import lax
from jax.sharding import PartitionSpec as P

decay_rate = 0.9
bf16 = jnp.bfloat16
f32 = jnp.float32


def slot_table(owner):
    count = owner.shape[0]
    earlier = lax.broadcasted_iota(jnp.int32, (count, count), 1) < lax.broadcasted_iota(
        jnp.int32, (count, count), 0
    )
    same = owner[:, None] == owner[None, :]
    return jnp.sum((same & earlier).astype(jnp.int32), axis=1)


def body(grads, owners, left, right, left_root, right_root):
    count, rows, order = grads.shape
    capacity = left.shape[1]
    workers = lax.axis_size("worker")
    shards = lax.axis_size("shard")
    part = order // workers
    w = lax.axis_index("worker")
    s = lax.axis_index("shard")
    owner = owners[:, 0]
    slot = slot_table(owner)
    flat = owner * capacity + slot
    spots = lax.broadcasted_iota(jnp.int32, (workers * capacity, count), 0)
    named = flat[None, :] == spots
    holder = jnp.argmax(named, axis=1).astype(jnp.int32)
    filled = lax.dynamic_slice_in_dim(jnp.any(named, axis=1), w * capacity, capacity)[
        :, None, None
    ]

    roots = jnp.concatenate([left_root, right_root], axis=0)
    row_ids = lax.broadcasted_iota(jnp.int32, roots.shape, 2) + s * rows
    on_diag = lax.broadcasted_iota(jnp.int32, roots.shape, 3) == row_ids
    diag = jnp.sum(jnp.where(on_diag, roots, 0.0), axis=3)
    diags = lax.all_gather(diag, ("shard", "worker"), axis=0, tiled=False)
    diags = diags.reshape(shards, workers, 2, capacity, rows)

    g_part = lax.dynamic_slice_in_dim(grads, w * part, part, 2)
    g_cols = lax.all_to_all(g_part, "shard", 0, 0, tiled=True).reshape(order, part)
    g_full = lax.all_gather(g_cols, "worker", axis=0, tiled=False)

    off = jnp.where(on_diag, 0.0, roots).astype(bf16)
    off = off.reshape(2, capacity, rows, workers, part).transpose(3, 1, 0, 2, 4)
    off = lax.all_to_all(off, "worker", 0, 0, tiled=True)
    off = off.reshape(workers * capacity, 2, rows, part)
    off = jnp.take(off, flat, axis=0)
    off = lax.all_to_all(off, "shard", 0, 0, tiled=True)
    l_cols = off[:, 0].reshape(order, part)
    r_cols = off[:, 1].reshape(order, part)
    l_full = lax.all_gather(l_cols, "worker", axis=0, tiled=False)

    my_flat = flat[s]
    my_diag = lax.dynamic_slice(
        diags,
        (0, my_flat // capacity, 0, my_flat % capacity, 0),
        (shards, 1, 2, 1, rows),
    ).reshape(shards, 2, rows)
    l_diag = my_diag[:, 0].reshape(order)
    r_diag = lax.dynamic_slice_in_dim(my_diag[:, 1].reshape(order), w * part, part)

    g_rows = lax.dynamic_slice_in_dim(g_full, w * part, part, 1)
    gram_left = jnp.einsum("vnk,vmk->nm", g_full, g_rows, preferred_element_type=f32)
    gram_right = jnp.einsum("vnk,nm->vkm", g_full, g_cols, preferred_element_type=f32)
    image = jnp.einsum(
        "vnk,vkm->nm", g_full, r_cols.reshape(workers, part, part), preferred_element_type=f32
    )
    image = (image + g_cols.astype(f32) * r_diag[None, :]).astype(bf16)
    result = jnp.einsum(
        "vnk,vkm->nm", l_full, image.reshape(workers, part, part), preferred_element_type=f32
    )
    result = (result + image.astype(f32) * l_diag[:, None]).astype(bf16)

    result = lax.all_to_all(result.reshape(shards, rows, part), "shard", 0, 0, tiled=True)
    precond = lax.all_gather(result, "worker", axis=2, tiled=True)

    grams = jnp.stack(
        [
            gram_left.astype(bf16).reshape(shards, rows, part),
            gram_right.astype(bf16).reshape(shards, rows, part),
        ],
        axis=1,
    )
    grams = lax.all_to_all(grams, "shard", 0, 0, tiled=True)
    grams = jnp.take(grams, holder, axis=0).reshape(workers, capacity, 2, rows, part)
    grams = lax.all_to_all(grams, "worker", 0, 0, tiled=True)
    grams = grams.transpose(2, 1, 3, 0, 4).reshape(2, capacity, rows, order).astype(f32)
    upd_left = jnp.where(filled, decay_rate * left[0] + (1.0 - decay_rate) * grams[0], left[0])
    upd_right = jnp.where(filled, decay_rate * right[0] + (1.0 - decay_rate) * grams[1], right[0])
    return (upd_left[None], upd_right[None], precond)


def solution(mesh):
    factor = P("worker", None, "shard", None)
    return jax.shard_map(
        body,
        mesh=mesh,
        in_specs=(P(None, "shard", None), P(), factor, factor, factor, factor),
        out_specs=(factor, factor, P(None, "shard", None)),
        check_vma=False,
    )
```

```python
import jax
import jax.numpy as jnp
from jax import lax
from jax.experimental import pallas as pl
from jax.experimental.pallas import tpu as pltpu
from jax.sharding import PartitionSpec as P

decay_rate = 0.9
bf16 = jnp.bfloat16
f32 = jnp.float32

BS = 1024
NB = 32
CAP = 6
ROWS = 32
NW = 8
PART = 128
PARTNERS = [(k, o) for k in range(4) for o in range(2)]
VMEM = pl.BlockSpec(memory_space=pltpu.VMEM)
SMEM = pl.BlockSpec(memory_space=pltpu.SMEM)


def partner(worker, k, other):
    core = worker % 2
    core = 1 - core if other else core
    return (worker // 2 + k) % 4 * 2 + core


def send(value, k, other):
    return lax.ppermute(value, "worker", [(w, partner(w, k, other)) for w in range(NW)])


def exchange(pieces):
    return [p if j == 0 else send(p, *PARTNERS[j]) for j, p in enumerate(pieces)]


def gather(piece):
    along = [piece] + [send(piece, k, 0) for k in range(1, 4)]
    out = []
    for p in along:
        out += [p, send(p, 0, 1)]
    return out


def sources(worker):
    return [partner(worker, 4 - k, other) for k, other in PARTNERS]


def dests(worker):
    return [partner(worker, k, other) for k, other in PARTNERS]


def call(kernel, outs, args, in_specs=None, out_specs=None, flops=0, nbytes=2 << 20):
    return pl.pallas_call(
        kernel,
        out_shape=outs,
        in_specs=in_specs or [VMEM] * len(args),
        out_specs=out_specs or jax.tree.map(lambda _: VMEM, outs),
        compiler_params=pltpu.CompilerParams(vmem_limit_bytes=20 << 20),
        cost_estimate=pl.CostEstimate(flops=flops, bytes_accessed=nbytes, transcendentals=0),
    )(*args)


def shape(dims, kind=bf16):
    return jax.ShapeDtypeStruct(dims, kind)


def pack_roots(owners, left, right, *outs):
    holder, outs = outs[-1], outs[:-1]
    worker, shard = lax.axis_index("worker"), lax.axis_index("shard")
    for i in range(NW * CAP):
        holder[i] = -1

    def name(b, carry):
        who = owners[b]
        taken = lax.fori_loop(
            0, CAP, lambda c, n: n + (holder[who * CAP + c] >= 0).astype(jnp.int32), 0
        )
        holder[who * CAP + taken] = b
        return carry

    lax.fori_loop(0, NB, name, 0)
    row = lax.broadcasted_iota(jnp.int32, (ROWS, PART), 0)
    lane = lax.broadcasted_iota(jnp.int32, (ROWS, PART), 1)
    near = shard // 4
    on_diag = lane == row + shard % 4 * ROWS
    diag_rows = []
    for c in range(CAP):
        total = jnp.zeros((1, PART), f32)
        for n, ref in enumerate((left, right)):
            block = ref[c, :, pl.ds(pl.multiple_of(near * PART, PART), PART)]
            d = jnp.sum(jnp.where(on_diag, block, 0.0), axis=0, keepdims=True)
            high = d.astype(bf16).astype(f32)
            for m, v in enumerate((high, d - high)):
                to = (2 * n + m) * ROWS
                total = total + pltpu.roll(v, (to + PART - shard % 4 * ROWS) % PART, 1)
        diag_rows.append(total)
    diag_tile = jnp.concatenate(diag_rows + [jnp.zeros((16 - CAP, PART), f32)], axis=0).astype(bf16)
    for out, to in zip(outs, dests(worker)):
        cols = pl.ds(pl.multiple_of(to * PART, PART), PART)
        mask = on_diag & (to == near)
        for c in range(CAP):
            for n, ref in enumerate((left, right)):
                at = (2 * c + n) * ROWS
                out[at : at + ROWS, :] = jnp.where(mask, 0.0, ref[c, :, cols]).astype(bf16)
        out[2 * CAP * ROWS :, :] = diag_tile


def pick_roots(holder, *refs):
    pieces, (out_left, out_right) = refs[:NW], refs[NW:]
    worker = lax.axis_index("worker")
    for piece, source in zip(pieces, sources(worker)):
        diag_tile = piece[2 * CAP * ROWS :, :].astype(f32)
        for c in range(CAP):
            block = holder[source * CAP + c]

            @pl.when(block >= 0)
            def _():
                out_left[block] = piece[2 * c * ROWS : (2 * c + 1) * ROWS, :]
                out_right[block, :ROWS, :] = piece[(2 * c + 1) * ROWS : (2 * c + 2) * ROWS, :]
                out_right[block, ROWS:, :] = jnp.broadcast_to(
                    diag_tile[c : c + 1], (16, PART)
                ).astype(bf16)


def make_grams(*refs):
    pieces, out = refs[:NW], refs[NW]
    worker = lax.axis_index("worker")
    mine = pl.ds(pl.multiple_of(worker * PART, PART), PART)
    total = jnp.zeros((BS, PART), f32)
    for piece, source in zip(pieces, sources(worker)):
        total = total + lax.dot_general(
            piece[...], piece[mine, :], (((1,), (1,)), ((), ())), preferred_element_type=f32
        )
        block = lax.dot_general(
            piece[...], pieces[0][...], (((0,), (0,)), ((), ())), preferred_element_type=f32
        )
        out[pl.ds(source * 4, 4), ROWS:, :] = block.astype(bf16).reshape(4, ROWS, PART)
    out[:, :ROWS, :] = total.astype(bf16).reshape(NB, ROWS, PART)


def make_image(right, *refs):
    pieces, out = refs[:NW], refs[NW]
    worker = lax.axis_index("worker")
    lane = lax.broadcasted_iota(jnp.int32, (1, PART), 1)
    diag = jnp.zeros((1, PART), f32)
    for q in range(4):
        d = right[worker * 4 + q, ROWS:, :].astype(f32)[:1]
        both = pltpu.roll(d, 64, 1) + pltpu.roll(d, 32, 1)
        diag = diag + pltpu.roll(jnp.where(lane < ROWS, both, 0.0), q * ROWS, 1)
    total = pieces[0][...].astype(f32) * diag
    for piece, source in zip(pieces, sources(worker)):
        block = right[pl.ds(source * 4, 4), :ROWS, :].reshape(PART, PART)
        total = total + jnp.dot(piece[...], block, preferred_element_type=f32)
    out[...] = total.astype(bf16)


def make_result(right, image, *refs):
    pieces, out = refs[:NW], refs[NW]
    worker = lax.axis_index("worker")
    diag_rows = right[:, ROWS:, :].astype(f32)[:, :1, :]
    row = lax.broadcasted_iota(jnp.int32, (NB, ROWS, PART), 1)
    lane = lax.broadcasted_iota(jnp.int32, (NB, ROWS, PART), 2)
    spread = jnp.where((lane == row) | (lane == row + ROWS), diag_rows, 0.0)
    spread = spread.astype(bf16).reshape(BS, PART)
    diag = jnp.dot(spread, jnp.ones((PART, PART), bf16), preferred_element_type=f32)
    total = image[...].astype(f32) * diag
    for piece, source in zip(pieces, sources(worker)):
        block = image[pl.ds(pl.multiple_of(source * PART, PART), PART), :]
        total = total + jnp.dot(piece[...], block, preferred_element_type=f32)
    out[...] = total.astype(bf16).reshape(NB, ROWS, PART)


def pack_grams(holder, grams, *outs):
    worker = lax.axis_index("worker")
    for out, to in zip(outs, dests(worker)):
        for c in range(CAP):
            block = holder[to * CAP + c]
            out[c] = grams[jnp.maximum(block, 0)]


def update(holder, left, right, *refs):
    pieces, outs = refs[:NW], refs[NW:]
    worker = lax.axis_index("worker")
    for c in range(CAP):
        filled = holder[worker * CAP + c] >= 0

        @pl.when(filled)
        def _():
            for piece, source in zip(pieces, sources(worker)):
                cols = pl.ds(pl.multiple_of(source * PART, PART), PART)
                for n, (old, new) in enumerate(zip((left, right), outs)):
                    gram = piece[c, n * ROWS : (n + 1) * ROWS, :].astype(f32)
                    new[c, :, cols] = decay_rate * old[c, :, cols] + (1.0 - decay_rate) * gram

        @pl.when(jnp.logical_not(filled))
        def _():
            for old, new in zip((left, right), outs):
                new[c] = old[c]


def assemble(*refs):
    pieces, out = refs[:NW], refs[NW]
    worker = lax.axis_index("worker")
    for piece, source in zip(pieces, sources(worker)):
        out[:, :, pl.ds(pl.multiple_of(source * PART, PART), PART)] = piece[...]


def over_shard(value):
    return lax.all_to_all(value, "shard", 0, 0, tiled=True)


def body(grads, owners, left, right, left_root, right_root):
    worker = lax.axis_index("worker")
    with jax.named_scope("roots"):
        *packed, holder = call(
            pack_roots,
            [shape((2 * CAP * ROWS + 16, PART))] * NW + [shape((NW * CAP,), jnp.int32)],
            (owners[:, 0], left_root[0], right_root[0]),
            [SMEM, VMEM, VMEM],
            [VMEM] * NW + [SMEM],
        )
        packed = exchange(packed)
    with jax.named_scope("gradients"):
        mine = lax.dynamic_slice_in_dim(grads, worker * PART, PART, 2)
        mine = over_shard(mine).reshape(BS, PART)
        columns = gather(mine)
    with jax.named_scope("roots"):
        root_l, root_r = call(
            pick_roots,
            [shape((NB, ROWS, PART)), shape((NB, ROWS + 16, PART))],
            (holder, *packed),
            [SMEM] + [VMEM] * NW,
        )
        root_l = over_shard(root_l).reshape(BS, PART)
        root_l = gather(root_l)
        root_r = over_shard(root_r)
    with jax.named_scope("grams"):
        grams = call(
            make_grams, shape((NB, 2 * ROWS, PART)), tuple(columns), flops=4 * BS * BS * PART
        )
        grams = over_shard(grams)
        grams = call(
            pack_grams,
            [shape((CAP, 2 * ROWS, PART))] * NW,
            (holder, grams),
            [SMEM, VMEM],
        )
        grams = exchange(grams)
    with jax.named_scope("precondition"):
        image = call(
            make_image, shape((BS, PART)), (root_r, *columns), flops=2 * BS * BS * PART
        )
        result = call(
            make_result,
            shape((NB, ROWS, PART)),
            (root_r, image, *root_l),
            flops=2 * BS * BS * PART,
        )
        result = gather(over_shard(result))
        precond = call(assemble, shape((NB, ROWS, BS)), tuple(result), nbytes=4 << 20)
    with jax.named_scope("factors"):
        factor = shape((CAP, ROWS, BS), f32)
        new_left, new_right = call(
            update,
            [factor, factor],
            (holder, left[0], right[0], *grams),
            [SMEM] + [VMEM] * (2 + NW),
        )
    return new_left[None], new_right[None], precond


def solution(mesh):
    factor = P("worker", None, "shard", None)
    return jax.shard_map(
        body,
        mesh=mesh,
        in_specs=(P(None, "shard", None), P(), factor, factor, factor, factor),
        out_specs=(factor, factor, P(None, "shard", None)),
        check_vma=False,
    )
```

```python
import jax
import jax.numpy as jnp
from jax import lax
from jax.experimental import pallas as pl
from jax.experimental.pallas import tpu as pltpu
from jax.sharding import PartitionSpec as P

decay_rate = 0.9
bf16 = jnp.bfloat16
f32 = jnp.float32

BS = 1024
NB = 32
CAP = 6
ROWS = 32
NW = 8
HALF = ROWS // 2
PART = 128
PARTNERS = [(k, o) for k in range(4) for o in range(2)]
ANY = pl.BlockSpec(memory_space=pl.ANY)
HBM = pl.BlockSpec(memory_space=pltpu.HBM)
VMEM = pl.BlockSpec(memory_space=pltpu.VMEM)
SMEM = pl.BlockSpec(memory_space=pltpu.SMEM)


def partner(worker, k, other):
    core = worker % 2
    core = 1 - core if other else core
    return (worker // 2 + k) % 4 * 2 + core


def send(value, k, other):
    return lax.ppermute(value, "worker", [(w, partner(w, k, other)) for w in range(NW)])


def exchange(pieces):
    return [p if j == 0 else send(p, *PARTNERS[j]) for j, p in enumerate(pieces)]


def gather(piece, own):
    out = [piece, send(own, 0, 1)]
    for p in [send(piece, k, 0) for k in range(1, 4)]:
        out += [p, send(p, 0, 1)]
    return out


def sources(worker):
    return [partner(worker, 4 - k, other) for k, other in PARTNERS]


def dests(worker):
    return [partner(worker, k, other) for k, other in PARTNERS]


def call(kernel, outs, args, in_specs=None, out_specs=None, scratch=(), flops=0, nbytes=2 << 20, vmem=16):
    return pl.pallas_call(
        kernel,
        out_shape=outs,
        in_specs=in_specs or [VMEM] * len(args),
        out_specs=out_specs or jax.tree.map(lambda _: VMEM, outs),
        scratch_shapes=scratch,
        compiler_params=pltpu.CompilerParams(vmem_limit_bytes=vmem << 20),
        cost_estimate=pl.CostEstimate(flops=flops, bytes_accessed=nbytes, transcendentals=0),
    )(*args)


def shape(dims, kind=bf16):
    return jax.ShapeDtypeStruct(dims, kind)


def pack_roots(owners, left_hbm, right_hbm, grads, *refs):
    outs, (columns, holder, left, right, taken, sems, cut) = refs[:NW], refs[NW:]
    shard, worker = lax.axis_index("shard"), lax.axis_index("worker")
    copies = [
        [
            pltpu.make_async_copy(far.at[c], near.at[c], sems.at[n, c])
            for n, (far, near) in enumerate(((left_hbm, left), (right_hbm, right)))
        ]
        for c in range(CAP)
    ]
    for pair in copies:
        for copy in pair:
            copy.start()
    mine = pl.ds(pl.multiple_of(worker * PART, PART), PART)
    copy_columns = pltpu.make_async_copy(grads.at[:, :, mine], columns, cut)
    copy_columns.start()
    for i in range(NW * CAP):
        holder[i] = -1
    for i in range(NW):
        taken[i] = 0

    def name(b, carry):
        who = owners[b]
        slot = taken[who]
        holder[who * CAP + slot] = b
        taken[who] = slot + 1
        return carry

    lax.fori_loop(0, NB, name, 0)
    row = lax.broadcasted_iota(jnp.int32, (ROWS, PART), 0)
    lane = lax.broadcasted_iota(jnp.int32, (ROWS, PART), 1)
    near = shard // 4
    on_diag = lane == row + shard % 4 * ROWS
    diag_rows = []
    for c in range(CAP):
        for copy in copies[c]:
            copy.wait()
        total = jnp.zeros((1, PART), f32)
        for n, ref in enumerate((left, right)):
            block = ref[c, :, pl.ds(pl.multiple_of(near * PART, PART), PART)]
            d = jnp.sum(jnp.where(on_diag, block, 0.0), axis=0, keepdims=True)
            high = d.astype(bf16).astype(f32)
            for m, v in enumerate((high, d - high)):
                to = (2 * n + m) * ROWS
                total = total + pltpu.roll(v, (to + PART - shard % 4 * ROWS) % PART, 1)
            for out, to in zip(outs, dests(worker)):
                block = ref[c, :, pl.ds(pl.multiple_of(to * PART, PART), PART)]
                block = jnp.where(on_diag & (to == near), 0.0, block)
                out[(2 * c + n) * ROWS : (2 * c + n + 1) * ROWS, :] = block.astype(bf16)
        diag_rows.append(total)
    diag_tile = jnp.concatenate(diag_rows + [jnp.zeros((16 - CAP, PART), f32)], axis=0).astype(bf16)
    for out in outs:
        out[2 * CAP * ROWS :, :] = diag_tile
    copy_columns.wait()


def pick_roots(holder, *refs):
    pieces, out = refs[:NW], refs[NW]
    worker = lax.axis_index("worker")
    for piece, source in zip(pieces, sources(worker)):
        diag_tile = piece[2 * CAP * ROWS :, :].astype(f32)
        for c in range(CAP):
            block = holder[source * CAP + c]

            @pl.when(block >= 0)
            def _():
                out[block, : 2 * ROWS, :] = piece[2 * c * ROWS : 2 * (c + 1) * ROWS, :]
                out[block, 2 * ROWS :, :] = jnp.broadcast_to(
                    diag_tile[c : c + 1], (HALF, PART)
                ).astype(bf16)


def make_grams(roots, columns, out, image):
    worker = lax.axis_index("worker")
    mine = pl.ds(pl.multiple_of(worker * PART, PART), PART)
    own = columns[worker]
    lane = lax.broadcasted_iota(jnp.int32, (1, PART), 1)
    diag = jnp.zeros((1, PART), f32)
    for q in range(4):
        d = roots[worker * 4 + q, 2 * ROWS :, :].astype(f32)[:1]
        both = pltpu.roll(d, 64, 1) + pltpu.roll(d, 32, 1)
        diag = diag + pltpu.roll(jnp.where(lane < ROWS, both, 0.0), q * ROWS, 1)
    product = own.astype(f32) * diag
    gram = jnp.zeros((BS, PART), f32)
    for w in range(NW):
        gram = gram + lax.dot_general(
            columns[w], columns[w, mine, :], (((1,), (1,)), ((), ())), preferred_element_type=f32
        )
        block = roots[w * 4 : (w + 1) * 4, ROWS : 2 * ROWS, :].reshape(PART, PART)
        product = product + jnp.dot(columns[w], block, preferred_element_type=f32)
        block = lax.dot_general(
            columns[w], own, (((0,), (0,)), ((), ())), preferred_element_type=f32
        )
        out[w * 4 : (w + 1) * 4, ROWS:, :] = block.astype(bf16).reshape(4, ROWS, PART)
    out[:, :ROWS, :] = gram.astype(bf16).reshape(NB, ROWS, PART)
    image[...] = product.astype(bf16)


def make_result(after, roots, image, left, out):
    diag_rows = roots[:, 2 * ROWS :, :].astype(f32)[:, :1, :]
    row = lax.broadcasted_iota(jnp.int32, (NB, ROWS, PART), 1)
    lane = lax.broadcasted_iota(jnp.int32, (NB, ROWS, PART), 2)
    spread = jnp.where((lane == row) | (lane == row + ROWS), diag_rows, 0.0)
    spread = spread.astype(bf16).reshape(BS, PART)
    diag = jnp.dot(spread, jnp.ones((PART, PART), bf16), preferred_element_type=f32)
    total = image[...].astype(f32) * diag
    for w in range(NW):
        total = total + jnp.dot(
            left[w].reshape(BS, PART),
            image[w * PART : (w + 1) * PART, :],
            preferred_element_type=f32,
        )
    out[...] = total.astype(bf16).reshape(NB, ROWS, PART)


def pack_grams(holder, grams, *outs):
    worker = lax.axis_index("worker")
    for out, to in zip(outs, dests(worker)):
        for c in range(CAP):
            out[c] = grams[jnp.maximum(holder[to * CAP + c], 0)]


def update(holder, left, right, *refs):
    pieces, outs, held, sems, out_sems = refs[:NW], refs[NW : NW + 2], *refs[NW + 2 :]
    worker = lax.axis_index("worker")
    into = [
        [pltpu.make_async_copy(far.at[c], held.at[n, c], sems.at[n, c]) for c in range(CAP)]
        for n, far in enumerate((left, right))
    ]
    back = [
        [pltpu.make_async_copy(held.at[n, c], far.at[c], out_sems.at[n, c]) for c in range(CAP)]
        for n, far in enumerate(outs)
    ]
    for copies in into:
        for copy in copies:
            copy.start()
    for n in range(2):
        for c in range(CAP):
            into[n][c].wait()

            @pl.when(holder[worker * CAP + c] >= 0)
            def _():
                for piece, source in zip(pieces, sources(worker)):
                    cols = pl.ds(pl.multiple_of(source * PART, PART), PART)
                    gram = piece[c, n * ROWS : (n + 1) * ROWS, :].astype(f32)
                    held[n, c, :, cols] = (
                        decay_rate * held[n, c, :, cols] + (1.0 - decay_rate) * gram
                    )

            back[n][c].start()
    for copies in back:
        for copy in copies:
            copy.wait()


def assemble(*refs):
    pieces, out, sems = refs[:NW], refs[NW], refs[NW + 1]
    copies = []
    for j, source in enumerate(sources(lax.axis_index("worker"))):
        cols = pl.ds(pl.multiple_of(source * PART, PART), PART)
        copies.append(pltpu.make_async_copy(pieces[j], out.at[:, :, cols], sems.at[j]))
    for copy in copies:
        copy.start()
    for copy in copies:
        copy.wait()


def over_shard(value):
    return lax.all_to_all(value, "shard", 0, 0, tiled=True)


def over_worker(value):
    return lax.all_gather(value, "worker", axis=0, tiled=False)


def body(grads, owners, left, right, left_root, right_root):
    tile = shape((NB, ROWS, PART))
    with jax.named_scope("roots"):
        *packed, mine, holder = call(
            pack_roots,
            [shape((2 * CAP * ROWS + HALF, PART))] * NW + [tile, shape((NW * CAP,), jnp.int32)],
            (owners[:, 0], left_root[0], right_root[0], grads),
            [SMEM, HBM, HBM, HBM],
            [VMEM] * (NW + 1) + [SMEM],
            [
                pltpu.VMEM((CAP, ROWS, BS), f32),
                pltpu.VMEM((CAP, ROWS, BS), f32),
                pltpu.SMEM((NW,), jnp.int32),
                pltpu.SemaphoreType.DMA((2, CAP)),
                pltpu.SemaphoreType.DMA,
            ],
            vmem=61,
        )
        mine, packed = lax.optimization_barrier((over_shard(mine), exchange(packed)))
    with jax.named_scope("gradients"):
        columns = over_worker(mine.reshape(BS, PART))
    with jax.named_scope("roots"):
        roots = call(
            pick_roots,
            shape((NB, 2 * ROWS + HALF, PART)),
            (holder, *packed),
            [SMEM] + [VMEM] * NW,
        )
        roots = over_shard(roots)
        root_l = over_worker(roots[:, :ROWS])
    with jax.named_scope("grams"):
        grams, image = call(
            make_grams,
            [shape((NB, 2 * ROWS, PART)), shape((BS, PART))],
            (roots, columns),
            flops=6 * BS * BS * PART,
        )
        grams = over_shard(grams)
        packed = call(
            pack_grams,
            [shape((CAP, 2 * ROWS, PART))] * NW,
            (holder, grams),
            [SMEM, VMEM],
        )
    with jax.named_scope("precondition"):
        result = call(
            make_result,
            tile,
            (packed[0], roots, image, root_l),
            [ANY] + [VMEM] * 3,
            flops=2 * BS * BS * PART,
        )
        result, packed = lax.optimization_barrier((over_shard(result), exchange(packed)))
    with jax.named_scope("factors"):
        factor = shape((CAP, ROWS, BS), f32)
        new_left, new_right = call(
            update,
            [factor, factor],
            (holder, left[0], right[0], *packed),
            [SMEM, HBM, HBM] + [VMEM] * NW,
            [HBM, HBM],
            [
                pltpu.VMEM((2, CAP, ROWS, BS), f32),
                pltpu.SemaphoreType.DMA((2, CAP)),
                pltpu.SemaphoreType.DMA((2, CAP)),
            ],
            nbytes=20 << 20,
            vmem=48,
        )
        own, new_left = lax.optimization_barrier((result, new_left))
    with jax.named_scope("precondition"):
        precond = call(
            assemble,
            shape((NB, ROWS, BS)),
            tuple(gather(result, own)),
            [VMEM] * NW,
            HBM,
            [pltpu.SemaphoreType.DMA((NW,))],
            nbytes=4 << 20,
        )
    return new_left[None], new_right[None], precond


def solution(mesh):
    factor = P("worker", None, "shard", None)
    return jax.shard_map(
        body,
        mesh=mesh,
        in_specs=(P(None, "shard", None), P(), factor, factor, factor, factor),
        out_specs=(factor, factor, P(None, "shard", None)),
        check_vma=False,
    )
```

```python
import jax
import jax.numpy as jnp
from jax import lax
from jax.experimental import pallas as pl
from jax.experimental.pallas import tpu as pltpu
from jax.sharding import PartitionSpec as P

decay_rate = 0.9
bf16 = jnp.bfloat16
f32 = jnp.float32

BS = 1024
NB = 32
CAP = 6
ROWS = 32
NW = 8
HALF = ROWS // 2
PART = 128
PARTNERS = [(k, o) for k in range(4) for o in range(2)]
ANY = pl.BlockSpec(memory_space=pl.ANY)
HBM = pl.BlockSpec(memory_space=pltpu.HBM)
VMEM = pl.BlockSpec(memory_space=pltpu.VMEM)
SMEM = pl.BlockSpec(memory_space=pltpu.SMEM)


def partner(worker, k, other):
    core = worker % 2
    core = 1 - core if other else core
    return (worker // 2 + k) % 4 * 2 + core


def send(value, k, other):
    return lax.ppermute(value, "worker", [(w, partner(w, k, other)) for w in range(NW)])


def exchange(pieces):
    return [p if j == 0 else send(p, *PARTNERS[j]) for j, p in enumerate(pieces)]


def gather(piece, own=None):
    own = piece if own is None else own
    out = [piece, send(own, 0, 1)]
    for p in [send(piece, k, 0) for k in range(1, 4)]:
        out += [p, send(p, 0, 1)]
    return out


def sources(worker):
    return [partner(worker, 4 - k, other) for k, other in PARTNERS]


def dests(worker):
    return [partner(worker, k, other) for k, other in PARTNERS]


def call(kernel, outs, args, in_specs=None, out_specs=None, scratch=(), flops=0, nbytes=2 << 20, vmem=16):
    return pl.pallas_call(
        kernel,
        out_shape=outs,
        in_specs=in_specs or [VMEM] * len(args),
        out_specs=out_specs or jax.tree.map(lambda _: VMEM, outs),
        scratch_shapes=scratch,
        compiler_params=pltpu.CompilerParams(vmem_limit_bytes=vmem << 20),
        cost_estimate=pl.CostEstimate(flops=flops, bytes_accessed=nbytes, transcendentals=0),
    )(*args)


def shape(dims, kind=bf16):
    return jax.ShapeDtypeStruct(dims, kind)


def pack_roots(owners, left_hbm, right_hbm, grads, *refs):
    outs, (columns, holder, left, right, taken, sems, cut) = refs[:NW], refs[NW:]
    shard, worker = lax.axis_index("shard"), lax.axis_index("worker")
    copies = [
        [
            pltpu.make_async_copy(far.at[c], near.at[c], sems.at[n, c])
            for n, (far, near) in enumerate(((left_hbm, left), (right_hbm, right)))
        ]
        for c in range(CAP)
    ]
    for pair in copies:
        for copy in pair:
            copy.start()
    mine = pl.ds(pl.multiple_of(worker * PART, PART), PART)
    copy_columns = pltpu.make_async_copy(grads.at[:, :, mine], columns, cut)
    copy_columns.start()
    for i in range(NW * CAP):
        holder[i] = -1
    for i in range(NW):
        taken[i] = 0

    def name(b, carry):
        who = owners[b]
        slot = taken[who]
        holder[who * CAP + slot] = b
        taken[who] = slot + 1
        return carry

    lax.fori_loop(0, NB, name, 0)
    row = lax.broadcasted_iota(jnp.int32, (ROWS, PART), 0)
    lane = lax.broadcasted_iota(jnp.int32, (ROWS, PART), 1)
    near = shard // 4
    on_diag = lane == row + shard % 4 * ROWS
    diag_rows = []
    for c in range(CAP):
        for copy in copies[c]:
            copy.wait()
        total = jnp.zeros((1, PART), f32)
        for n, ref in enumerate((left, right)):
            block = ref[c, :, pl.ds(pl.multiple_of(near * PART, PART), PART)]
            d = jnp.sum(jnp.where(on_diag, block, 0.0), axis=0, keepdims=True)
            high = d.astype(bf16).astype(f32)
            for m, v in enumerate((high, d - high)):
                to = (2 * n + m) * ROWS
                total = total + pltpu.roll(v, (to + PART - shard % 4 * ROWS) % PART, 1)
            for out, to in zip(outs, dests(worker)):
                block = ref[c, :, pl.ds(pl.multiple_of(to * PART, PART), PART)]
                block = jnp.where(on_diag & (to == near), 0.0, block)
                out[(2 * c + n) * ROWS : (2 * c + n + 1) * ROWS, :] = block.astype(bf16)
        diag_rows.append(total)
    diag_tile = jnp.concatenate(diag_rows + [jnp.zeros((16 - CAP, PART), f32)], axis=0).astype(bf16)
    for out in outs:
        out[2 * CAP * ROWS :, :] = diag_tile
    copy_columns.wait()


def pick_roots(holder, *refs):
    pieces, out = refs[:NW], refs[NW]
    worker = lax.axis_index("worker")
    for piece, source in zip(pieces, sources(worker)):
        diag_tile = piece[2 * CAP * ROWS :, :].astype(f32)
        for c in range(CAP):
            block = holder[source * CAP + c]

            @pl.when(block >= 0)
            def _():
                out[block, : 2 * ROWS, :] = piece[2 * c * ROWS : 2 * (c + 1) * ROWS, :]
                out[block, 2 * ROWS :, :] = jnp.broadcast_to(
                    diag_tile[c : c + 1], (HALF, PART)
                ).astype(bf16)


def make_grams(roots, *refs):
    pieces, (out, image) = refs[:NW], refs[NW:]
    worker = lax.axis_index("worker")
    mine = pl.ds(pl.multiple_of(worker * PART, PART), PART)
    own = pieces[0][...]
    lane = lax.broadcasted_iota(jnp.int32, (1, PART), 1)
    diag = jnp.zeros((1, PART), f32)
    for q in range(4):
        d = roots[worker * 4 + q, 2 * ROWS :, :].astype(f32)[:1]
        both = pltpu.roll(d, 64, 1) + pltpu.roll(d, 32, 1)
        diag = diag + pltpu.roll(jnp.where(lane < ROWS, both, 0.0), q * ROWS, 1)
    product = own.astype(f32) * diag
    gram = jnp.zeros((BS, PART), f32)
    for piece, source in zip(pieces, sources(worker)):
        columns = piece[...]
        gram = gram + lax.dot_general(
            columns, piece[mine, :], (((1,), (1,)), ((), ())), preferred_element_type=f32
        )
        block = roots[pl.ds(source * 4, 4), ROWS : 2 * ROWS, :].reshape(PART, PART)
        product = product + jnp.dot(columns, block, preferred_element_type=f32)
        block = lax.dot_general(columns, own, (((0,), (0,)), ((), ())), preferred_element_type=f32)
        out[pl.ds(source * 4, 4), ROWS:, :] = block.astype(bf16).reshape(4, ROWS, PART)
    out[:, :ROWS, :] = gram.astype(bf16).reshape(NB, ROWS, PART)
    image[...] = product.astype(bf16)


def make_result(roots, image, *refs):
    pieces, out = refs[:NW], refs[NW]
    diag_rows = roots[:, 2 * ROWS :, :].astype(f32)[:, :1, :]
    row = lax.broadcasted_iota(jnp.int32, (NB, ROWS, PART), 1)
    lane = lax.broadcasted_iota(jnp.int32, (NB, ROWS, PART), 2)
    spread = jnp.where((lane == row) | (lane == row + ROWS), diag_rows, 0.0)
    spread = spread.astype(bf16).reshape(BS, PART)
    diag = jnp.dot(spread, jnp.ones((PART, PART), bf16), preferred_element_type=f32)
    total = image[...].astype(f32) * diag
    for piece, source in zip(pieces, sources(lax.axis_index("worker"))):
        block = image[pl.ds(pl.multiple_of(source * PART, PART), PART), :]
        total = total + jnp.dot(piece[...], block, preferred_element_type=f32)
    out[...] = total.astype(bf16).reshape(NB, ROWS, PART)


def pack_grams(holder, grams, *outs):
    worker = lax.axis_index("worker")
    for out, to in zip(outs, dests(worker)):
        for c in range(CAP):
            out[c] = grams[jnp.maximum(holder[to * CAP + c], 0)]


def update(holder, left, right, *refs):
    pieces, outs, held, sems, out_sems = refs[:NW], refs[NW : NW + 2], *refs[NW + 2 :]
    worker = lax.axis_index("worker")
    into = [
        [pltpu.make_async_copy(far.at[c], held.at[n, c], sems.at[n, c]) for c in range(CAP)]
        for n, far in enumerate((left, right))
    ]
    back = [
        [pltpu.make_async_copy(held.at[n, c], far.at[c], out_sems.at[n, c]) for c in range(CAP)]
        for n, far in enumerate(outs)
    ]
    for copies in into:
        for copy in copies:
            copy.start()
    for n in range(2):
        for c in range(CAP):
            into[n][c].wait()

            @pl.when(holder[worker * CAP + c] >= 0)
            def _():
                for piece, source in zip(pieces, sources(worker)):
                    cols = pl.ds(pl.multiple_of(source * PART, PART), PART)
                    gram = piece[c, n * ROWS : (n + 1) * ROWS, :].astype(f32)
                    held[n, c, :, cols] = (
                        decay_rate * held[n, c, :, cols] + (1.0 - decay_rate) * gram
                    )

            back[n][c].start()
    for copies in back:
        for copy in copies:
            copy.wait()


def assemble(*refs):
    pieces, out, sems = refs[:NW], refs[NW], refs[NW + 1]
    copies = []
    for j, source in enumerate(sources(lax.axis_index("worker"))):
        cols = pl.ds(pl.multiple_of(source * PART, PART), PART)
        copies.append(pltpu.make_async_copy(pieces[j], out.at[:, :, cols], sems.at[j]))
    for copy in copies:
        copy.start()
    for copy in copies:
        copy.wait()


def over_shard(value):
    return lax.all_to_all(value, "shard", 0, 0, tiled=True)


def body(grads, owners, left, right, left_root, right_root):
    tile = shape((NB, ROWS, PART))
    with jax.named_scope("roots"):
        *packed, mine, holder = call(
            pack_roots,
            [shape((2 * CAP * ROWS + HALF, PART))] * NW + [tile, shape((NW * CAP,), jnp.int32)],
            (owners[:, 0], left_root[0], right_root[0], grads),
            [SMEM, HBM, HBM, HBM],
            [VMEM] * (NW + 1) + [SMEM],
            [
                pltpu.VMEM((CAP, ROWS, BS), f32),
                pltpu.VMEM((CAP, ROWS, BS), f32),
                pltpu.SMEM((NW,), jnp.int32),
                pltpu.SemaphoreType.DMA((2, CAP)),
                pltpu.SemaphoreType.DMA,
            ],
            vmem=61,
        )
        mine, packed = lax.optimization_barrier((over_shard(mine), exchange(packed)))
    with jax.named_scope("gradients"):
        columns = gather(mine.reshape(BS, PART))
    with jax.named_scope("roots"):
        roots = call(
            pick_roots,
            shape((NB, 2 * ROWS + HALF, PART)),
            (holder, *packed),
            [SMEM] + [VMEM] * NW,
        )
        roots, columns = lax.optimization_barrier((over_shard(roots), columns))
        root_l = gather(roots[:, :ROWS].reshape(BS, PART))
    with jax.named_scope("grams"):
        grams, image = call(
            make_grams,
            [shape((NB, 2 * ROWS, PART)), shape((BS, PART))],
            (roots, *columns),
            flops=6 * BS * BS * PART,
        )
        grams, root_l = lax.optimization_barrier((over_shard(grams), root_l))
        packed = call(
            pack_grams,
            [shape((CAP, 2 * ROWS, PART))] * NW,
            (holder, grams),
            [SMEM, VMEM],
        )
    with jax.named_scope("precondition"):
        result = call(
            make_result,
            tile,
            (roots, image, *root_l),
            flops=2 * BS * BS * PART,
        )
        result, packed = lax.optimization_barrier((over_shard(result), exchange(packed)))
    with jax.named_scope("factors"):
        factor = shape((CAP, ROWS, BS), f32)
        new_left, new_right = call(
            update,
            [factor, factor],
            (holder, left[0], right[0], *packed),
            [SMEM, HBM, HBM] + [VMEM] * NW,
            [HBM, HBM],
            [
                pltpu.VMEM((2, CAP, ROWS, BS), f32),
                pltpu.SemaphoreType.DMA((2, CAP)),
                pltpu.SemaphoreType.DMA((2, CAP)),
            ],
            nbytes=20 << 20,
            vmem=61,
        )
        own, new_left = lax.optimization_barrier((result, new_left))
    with jax.named_scope("precondition"):
        precond = call(
            assemble,
            shape((NB, ROWS, BS)),
            tuple(gather(result, own)),
            [VMEM] * NW,
            HBM,
            [pltpu.SemaphoreType.DMA((NW,))],
            nbytes=4 << 20,
        )
    return new_left[None], new_right[None], precond


def solution(mesh):
    factor = P("worker", None, "shard", None)
    return jax.shard_map(
        body,
        mesh=mesh,
        in_specs=(P(None, "shard", None), P(), factor, factor, factor, factor),
        out_specs=(factor, factor, P(None, "shard", None)),
        check_vma=False,
    )
```

```python
import jax
import jax.numpy as jnp
from jax import lax
from jax.experimental import pallas as pl
from jax.experimental.pallas import tpu as pltpu
from jax.sharding import PartitionSpec as P

decay_rate = 0.9
bf16 = jnp.bfloat16
f32 = jnp.float32

BS = 1024
NB = 32
CAP = 6
ROWS = 32
NW = 8
HALF = ROWS // 2
PART = 128
PARTNERS = [(k, o) for k in range(4) for o in range(2)]
ANY = pl.BlockSpec(memory_space=pl.ANY)
HBM = pl.BlockSpec(memory_space=pltpu.HBM)
VMEM = pl.BlockSpec(memory_space=pltpu.VMEM)
SMEM = pl.BlockSpec(memory_space=pltpu.SMEM)


def partner(worker, k, other):
    core = worker % 2
    core = 1 - core if other else core
    return (worker // 2 + k) % 4 * 2 + core


def send(value, k, other):
    return lax.ppermute(value, "worker", [(w, partner(w, k, other)) for w in range(NW)])


def exchange(pieces):
    return [p if j == 0 else send(p, *PARTNERS[j]) for j, p in enumerate(pieces)]


def outgoing(refs):
    own, given, *pairs = refs
    return [own, given] + [pair.at[o] for pair in pairs for o in range(2)]


def incoming(refs):
    return list(refs[:2]) + [ref.at[j % 2] for j, ref in enumerate(refs[2:])]


def gather(piece, own=None):
    own = piece if own is None else own
    out = [piece, send(own, 0, 1)]
    for p in [send(piece, k, 0) for k in range(1, 4)]:
        out += [p, send(p, 0, 1)]
    return out


def sources(worker):
    return [partner(worker, 4 - k, other) for k, other in PARTNERS]


def dests(worker):
    return [partner(worker, k, other) for k, other in PARTNERS]


def call(kernel, outs, args, in_specs=None, out_specs=None, scratch=(), flops=0, nbytes=2 << 20, vmem=16):
    return pl.pallas_call(
        kernel,
        out_shape=outs,
        in_specs=in_specs or [VMEM] * len(args),
        out_specs=out_specs or jax.tree.map(lambda _: VMEM, outs),
        scratch_shapes=scratch,
        compiler_params=pltpu.CompilerParams(vmem_limit_bytes=vmem << 20),
        cost_estimate=pl.CostEstimate(flops=flops, bytes_accessed=nbytes, transcendentals=0),
    )(*args)


def shape(dims, kind=bf16):
    return jax.ShapeDtypeStruct(dims, kind)


def pack_roots(owners, left_hbm, right_hbm, grads, *refs):
    outs, (columns, holder, left, right, taken, sems, cut) = refs[:NW], refs[NW:]
    shard, worker = lax.axis_index("shard"), lax.axis_index("worker")
    copies = [
        [
            pltpu.make_async_copy(far.at[c], near.at[c], sems.at[n, c])
            for n, (far, near) in enumerate(((left_hbm, left), (right_hbm, right)))
        ]
        for c in range(CAP)
    ]
    for pair in copies:
        for copy in pair:
            copy.start()
    mine = pl.ds(pl.multiple_of(worker * PART, PART), PART)
    column_copies = [
        pltpu.make_async_copy(grads.at[4 * i : 4 * i + 4, :, mine], columns.at[4 * i : 4 * i + 4], cut.at[i])
        for i in range(NB // 4)
    ]
    for copy in column_copies:
        copy.start()
    for i in range(NW * CAP):
        holder[i] = -1
    for i in range(NW):
        taken[i] = 0

    def name(b, carry):
        who = owners[b]
        slot = taken[who]
        holder[who * CAP + slot] = b
        taken[who] = slot + 1
        return carry

    lax.fori_loop(0, NB, name, 0)
    row = lax.broadcasted_iota(jnp.int32, (ROWS, PART), 0)
    lane = lax.broadcasted_iota(jnp.int32, (ROWS, PART), 1)
    near = shard // 4
    on_diag = lane == row + shard % 4 * ROWS
    diag_rows = []
    for c in range(CAP):
        for copy in copies[c]:
            copy.wait()
        total = jnp.zeros((1, PART), f32)
        for n, ref in enumerate((left, right)):
            block = ref[c, :, pl.ds(pl.multiple_of(near * PART, PART), PART)]
            d = jnp.sum(jnp.where(on_diag, block, 0.0), axis=0, keepdims=True)
            high = d.astype(bf16).astype(f32)
            for m, v in enumerate((high, d - high)):
                to = (2 * n + m) * ROWS
                total = total + pltpu.roll(v, (to + PART - shard % 4 * ROWS) % PART, 1)
            for out, to in zip(outs, dests(worker)):
                block = ref[c, :, pl.ds(pl.multiple_of(to * PART, PART), PART)]
                block = jnp.where(on_diag & (to == near), 0.0, block)
                out[(2 * c + n) * ROWS : (2 * c + n + 1) * ROWS, :] = block.astype(bf16)
        diag_rows.append(total)
    diag_tile = jnp.concatenate(diag_rows + [jnp.zeros((16 - CAP, PART), f32)], axis=0).astype(bf16)
    for out in outs:
        out[2 * CAP * ROWS :, :] = diag_tile
    for copy in column_copies:
        copy.wait()


def pick_roots(holder, *refs):
    pieces, out = refs[:NW], refs[NW]
    worker = lax.axis_index("worker")
    for piece, source in zip(pieces, sources(worker)):
        diag_tile = piece[2 * CAP * ROWS :, :].astype(f32)
        for c in range(CAP):
            block = holder[source * CAP + c]

            @pl.when(block >= 0)
            def _():
                out[block, : 2 * ROWS, :] = piece[2 * c * ROWS : 2 * (c + 1) * ROWS, :]
                out[block, 2 * ROWS :, :] = jnp.broadcast_to(
                    diag_tile[c : c + 1], (HALF, PART)
                ).astype(bf16)


def make_grams(roots, *refs):
    pieces, (out, image) = refs[:NW], refs[NW:]
    worker = lax.axis_index("worker")
    mine = pl.ds(pl.multiple_of(worker * PART, PART), PART)
    own = pieces[0][...]
    lane = lax.broadcasted_iota(jnp.int32, (1, PART), 1)
    diag = jnp.zeros((1, PART), f32)
    for q in range(4):
        d = roots[worker * 4 + q, 2 * ROWS :, :].astype(f32)[:1]
        both = pltpu.roll(d, 64, 1) + pltpu.roll(d, 32, 1)
        diag = diag + pltpu.roll(jnp.where(lane < ROWS, both, 0.0), q * ROWS, 1)
    product = own.astype(f32) * diag
    gram = jnp.zeros((BS, PART), f32)
    for piece, source in zip(pieces, sources(worker)):
        columns = piece[...]
        gram = gram + lax.dot_general(
            columns, piece[mine, :], (((1,), (1,)), ((), ())), preferred_element_type=f32
        )
        block = roots[pl.ds(source * 4, 4), ROWS : 2 * ROWS, :].reshape(PART, PART)
        product = product + jnp.dot(columns, block, preferred_element_type=f32)
        block = lax.dot_general(columns, own, (((0,), (0,)), ((), ())), preferred_element_type=f32)
        out[pl.ds(source * 4, 4), ROWS:, :] = block.astype(bf16).reshape(4, ROWS, PART)
    out[:, :ROWS, :] = gram.astype(bf16).reshape(NB, ROWS, PART)
    image[...] = product.astype(bf16)


def make_result(roots, image, *refs):
    pieces, out = refs[:NW], refs[NW]
    diag_rows = roots[:, 2 * ROWS :, :].astype(f32)[:, :1, :]
    row = lax.broadcasted_iota(jnp.int32, (NB, ROWS, PART), 1)
    lane = lax.broadcasted_iota(jnp.int32, (NB, ROWS, PART), 2)
    spread = jnp.where((lane == row) | (lane == row + ROWS), diag_rows, 0.0)
    spread = spread.astype(bf16).reshape(BS, PART)
    diag = jnp.dot(spread, jnp.ones((PART, PART), bf16), preferred_element_type=f32)
    total = image[...].astype(f32) * diag
    for piece, source in zip(pieces, sources(lax.axis_index("worker"))):
        block = image[pl.ds(pl.multiple_of(source * PART, PART), PART), :]
        total = total + jnp.dot(piece[...], block, preferred_element_type=f32)
    out[...] = total.astype(bf16).reshape(NB, ROWS, PART)


def pack_grams(holder, grams, *outs):
    worker = lax.axis_index("worker")
    for out, to in zip(outgoing(outs), dests(worker)):
        for c in range(CAP):
            out[c] = grams[jnp.maximum(holder[to * CAP + c], 0)]


def update(holder, left, right, *refs):
    pieces, outs, held, sems, out_sems = incoming(refs[:NW]), refs[NW : NW + 2], *refs[NW + 2 :]
    worker = lax.axis_index("worker")
    into = [
        [pltpu.make_async_copy(far.at[c], held.at[n, c], sems.at[n, c]) for c in range(CAP)]
        for n, far in enumerate((left, right))
    ]
    back = [
        [pltpu.make_async_copy(held.at[n, c], far.at[c], out_sems.at[n, c]) for c in range(CAP)]
        for n, far in enumerate(outs)
    ]
    for copies in into:
        for copy in copies:
            copy.start()
    for n in range(2):
        for c in range(CAP):
            into[n][c].wait()

            @pl.when(holder[worker * CAP + c] >= 0)
            def _():
                for piece, source in zip(pieces, sources(worker)):
                    cols = pl.ds(pl.multiple_of(source * PART, PART), PART)
                    gram = piece[c, n * ROWS : (n + 1) * ROWS, :].astype(f32)
                    held[n, c, :, cols] = (
                        decay_rate * held[n, c, :, cols] + (1.0 - decay_rate) * gram
                    )

            back[n][c].start()
    for copies in back:
        for copy in copies:
            copy.wait()


def assemble(*refs):
    pieces, out, sems = refs[:NW], refs[NW], refs[NW + 1]
    copies = []
    for j, source in enumerate(sources(lax.axis_index("worker"))):
        cols = pl.ds(pl.multiple_of(source * PART, PART), PART)
        copies.append(pltpu.make_async_copy(pieces[j], out.at[:, :, cols], sems.at[j]))
    for copy in copies:
        copy.start()
    for copy in copies:
        copy.wait()


def over_shard(value):
    return lax.all_to_all(value, "shard", 0, 0, tiled=True)


def body(grads, owners, left, right, left_root, right_root):
    tile = shape((NB, ROWS, PART))
    with jax.named_scope("roots"):
        *packed, mine, holder = call(
            pack_roots,
            [shape((2 * CAP * ROWS + HALF, PART))] * NW + [tile, shape((NW * CAP,), jnp.int32)],
            (owners[:, 0], left_root[0], right_root[0], grads),
            [SMEM, HBM, HBM, HBM],
            [VMEM] * (NW + 1) + [SMEM],
            [
                pltpu.VMEM((CAP, ROWS, BS), f32),
                pltpu.VMEM((CAP, ROWS, BS), f32),
                pltpu.SMEM((NW,), jnp.int32),
                pltpu.SemaphoreType.DMA((2, CAP)),
                pltpu.SemaphoreType.DMA((NB // 4,)),
            ],
            vmem=61,
        )
        mine, packed = lax.optimization_barrier((over_shard(mine), exchange(packed)))
    with jax.named_scope("gradients"):
        columns = gather(mine.reshape(BS, PART))
    with jax.named_scope("roots"):
        roots = call(
            pick_roots,
            shape((NB, 2 * ROWS + HALF, PART)),
            (holder, *packed),
            [SMEM] + [VMEM] * NW,
            vmem=61,
        )
        roots = over_shard(roots)
        root_l = gather(roots[:, :ROWS].reshape(BS, PART))
    with jax.named_scope("grams"):
        grams, image = call(
            make_grams,
            [shape((NB, 2 * ROWS, PART)), shape((BS, PART))],
            (roots, *columns),
            flops=6 * BS * BS * PART,
        )
        grams, root_l = lax.optimization_barrier((over_shard(grams), root_l))
        packed = call(
            pack_grams,
            [shape((CAP, 2 * ROWS, PART))] * 2 + [shape((2, CAP, 2 * ROWS, PART))] * 3,
            (holder, grams),
            [SMEM, VMEM],
        )
    with jax.named_scope("precondition"):
        result = call(
            make_result,
            tile,
            (roots, image, *root_l),
            flops=2 * BS * BS * PART,
        )
        own, given, *pairs = packed
        pairs = [send(pair, k, 0) for k, pair in enumerate(pairs, 1)]
        result, pairs, given = lax.optimization_barrier((over_shard(result), pairs, given))
        packed = [own, send(given, 0, 1)]
        for pair in pairs:
            packed += [pair, send(pair, 0, 1)]
    with jax.named_scope("factors"):
        factor = shape((CAP, ROWS, BS), f32)
        new_left, new_right = call(
            update,
            [factor, factor],
            (holder, left[0], right[0], *packed),
            [SMEM, HBM, HBM] + [VMEM] * NW,
            [HBM, HBM],
            [
                pltpu.VMEM((2, CAP, ROWS, BS), f32),
                pltpu.SemaphoreType.DMA((2, CAP)),
                pltpu.SemaphoreType.DMA((2, CAP)),
            ],
            nbytes=20 << 20,
            vmem=61,
        )
        own, new_left = lax.optimization_barrier((result, new_left))
    with jax.named_scope("precondition"):
        precond = call(
            assemble,
            shape((NB, ROWS, BS)),
            tuple(gather(result, own)),
            [VMEM] * NW,
            HBM,
            [pltpu.SemaphoreType.DMA((NW,))],
            nbytes=4 << 20,
        )
    return new_left[None], new_right[None], precond


def solution(mesh):
    factor = P("worker", None, "shard", None)
    return jax.shard_map(
        body,
        mesh=mesh,
        in_specs=(P(None, "shard", None), P(), factor, factor, factor, factor),
        out_specs=(factor, factor, P(None, "shard", None)),
        check_vma=False,
    )
```

```python
import jax
import jax.numpy as jnp
from jax import lax
from jax.experimental import pallas as pl
from jax.experimental.pallas import tpu as pltpu
from jax.sharding import PartitionSpec as P

decay_rate = 0.9
bf16 = jnp.bfloat16
f32 = jnp.float32

BS = 1024
NB = 32
CAP = 6
ROWS = 32
NW = 8
HALF = ROWS // 2
PART = 128
PARTNERS = [(k, o) for k in range(4) for o in range(2)]
ANY = pl.BlockSpec(memory_space=pl.ANY)
HBM = pl.BlockSpec(memory_space=pltpu.HBM)
VMEM = pl.BlockSpec(memory_space=pltpu.VMEM)
SMEM = pl.BlockSpec(memory_space=pltpu.SMEM)


def partner(worker, k, other):
    core = worker % 2
    core = 1 - core if other else core
    return (worker // 2 + k) % 4 * 2 + core


def send(value, k, other):
    return lax.ppermute(value, "worker", [(w, partner(w, k, other)) for w in range(NW)])


def exchange(pieces):
    return [p if j == 0 else send(p, *PARTNERS[j]) for j, p in enumerate(pieces)]


def outgoing(refs):
    own, given, *pairs = refs
    return [own, given] + [pair.at[o] for pair in pairs for o in range(2)]


def incoming(refs):
    return list(refs[:2]) + [ref.at[j % 2] for j, ref in enumerate(refs[2:])]


def gather(piece, own=None):
    own = piece if own is None else own
    out = [piece, send(own, 0, 1)]
    for p in [send(piece, k, 0) for k in range(1, 4)]:
        out += [p, send(p, 0, 1)]
    return out


def sources(worker):
    return [partner(worker, 4 - k, other) for k, other in PARTNERS]


def dests(worker):
    return [partner(worker, k, other) for k, other in PARTNERS]


def call(kernel, outs, args, in_specs=None, out_specs=None, scratch=(), flops=0, nbytes=2 << 20, vmem=16):
    return pl.pallas_call(
        kernel,
        out_shape=outs,
        in_specs=in_specs or [VMEM] * len(args),
        out_specs=out_specs or jax.tree.map(lambda _: VMEM, outs),
        scratch_shapes=scratch,
        compiler_params=pltpu.CompilerParams(vmem_limit_bytes=vmem << 20),
        cost_estimate=pl.CostEstimate(flops=flops, bytes_accessed=nbytes, transcendentals=0),
    )(*args)


def shape(dims, kind=bf16):
    return jax.ShapeDtypeStruct(dims, kind)


def pack_roots(owners, left_hbm, right_hbm, grads, *refs):
    outs, (columns, holder, left, right, taken, sems, cut) = refs[:NW], refs[NW:]
    shard, worker = lax.axis_index("shard"), lax.axis_index("worker")
    copies = [
        [
            pltpu.make_async_copy(far.at[c], near.at[c], sems.at[n, c])
            for n, (far, near) in enumerate(((left_hbm, left), (right_hbm, right)))
        ]
        for c in range(CAP)
    ]
    for pair in copies:
        for copy in pair:
            copy.start()
    mine = pl.ds(pl.multiple_of(worker * PART, PART), PART)
    column_copies = [
        pltpu.make_async_copy(grads.at[4 * i : 4 * i + 4, :, mine], columns.at[4 * i : 4 * i + 4], cut.at[i])
        for i in range(NB // 4)
    ]
    for copy in column_copies:
        copy.start()
    for i in range(NW * CAP):
        holder[i] = -1
    for i in range(NW):
        taken[i] = 0

    def name(b, carry):
        who = owners[b]
        slot = taken[who]
        holder[who * CAP + slot] = b
        taken[who] = slot + 1
        return carry

    lax.fori_loop(0, NB, name, 0)
    row = lax.broadcasted_iota(jnp.int32, (ROWS, PART), 0)
    lane = lax.broadcasted_iota(jnp.int32, (ROWS, PART), 1)
    near = shard // 4
    on_diag = lane == row + shard % 4 * ROWS
    diag_rows = []
    for c in range(CAP):
        for copy in copies[c]:
            copy.wait()
        total = jnp.zeros((1, PART), f32)
        for n, ref in enumerate((left, right)):
            block = ref[c, :, pl.ds(pl.multiple_of(near * PART, PART), PART)]
            d = jnp.sum(jnp.where(on_diag, block, 0.0), axis=0, keepdims=True)
            high = d.astype(bf16).astype(f32)
            for m, v in enumerate((high, d - high)):
                to = (2 * n + m) * ROWS
                total = total + pltpu.roll(v, (to + PART - shard % 4 * ROWS) % PART, 1)
            for out, to in zip(outs, dests(worker)):
                block = ref[c, :, pl.ds(pl.multiple_of(to * PART, PART), PART)]
                block = jnp.where(on_diag & (to == near), 0.0, block)
                out[(2 * c + n) * ROWS : (2 * c + n + 1) * ROWS, :] = block.astype(bf16)
        diag_rows.append(total)
    diag_tile = jnp.concatenate(diag_rows + [jnp.zeros((16 - CAP, PART), f32)], axis=0).astype(bf16)
    for out in outs:
        out[2 * CAP * ROWS :, :] = diag_tile
    for copy in column_copies:
        copy.wait()


def pick_roots(holder, *refs):
    pieces, out = refs[:NW], refs[NW]
    worker = lax.axis_index("worker")
    for piece, source in zip(pieces, sources(worker)):
        diag_tile = piece[2 * CAP * ROWS :, :].astype(f32)
        for c in range(CAP):
            block = holder[source * CAP + c]

            @pl.when(block >= 0)
            def _():
                out[block, : 2 * ROWS, :] = piece[2 * c * ROWS : 2 * (c + 1) * ROWS, :]
                out[block, 2 * ROWS :, :] = jnp.broadcast_to(
                    diag_tile[c : c + 1], (HALF, PART)
                ).astype(bf16)


def make_grams(roots, *refs):
    pieces, (out, image) = refs[:NW], refs[NW:]
    worker = lax.axis_index("worker")
    mine = pl.ds(pl.multiple_of(worker * PART, PART), PART)
    own = pieces[0][...]
    lane = lax.broadcasted_iota(jnp.int32, (1, PART), 1)
    diag = jnp.zeros((1, PART), f32)
    for q in range(4):
        d = roots[worker * 4 + q, 2 * ROWS :, :].astype(f32)[:1]
        both = pltpu.roll(d, 64, 1) + pltpu.roll(d, 32, 1)
        diag = diag + pltpu.roll(jnp.where(lane < ROWS, both, 0.0), q * ROWS, 1)
    product = own.astype(f32) * diag
    gram = jnp.zeros((BS, PART), f32)
    for piece, source in zip(pieces, sources(worker)):
        columns = piece[...]
        gram = gram + lax.dot_general(
            columns, piece[mine, :], (((1,), (1,)), ((), ())), preferred_element_type=f32
        )
        block = roots[pl.ds(source * 4, 4), ROWS : 2 * ROWS, :].reshape(PART, PART)
        product = product + jnp.dot(columns, block, preferred_element_type=f32)
        block = lax.dot_general(columns, own, (((0,), (0,)), ((), ())), preferred_element_type=f32)
        out[pl.ds(source * 4, 4), ROWS:, :] = block.astype(bf16).reshape(4, ROWS, PART)
    out[:, :ROWS, :] = gram.astype(bf16).reshape(NB, ROWS, PART)
    image[...] = product.astype(bf16)


def make_result(roots, image, *refs):
    pieces, out = refs[:NW], refs[NW]
    diag_rows = roots[:, 2 * ROWS :, :].astype(f32)[:, :1, :]
    row = lax.broadcasted_iota(jnp.int32, (NB, ROWS, PART), 1)
    lane = lax.broadcasted_iota(jnp.int32, (NB, ROWS, PART), 2)
    spread = jnp.where((lane == row) | (lane == row + ROWS), diag_rows, 0.0)
    spread = spread.astype(bf16).reshape(BS, PART)
    diag = jnp.dot(spread, jnp.ones((PART, PART), bf16), preferred_element_type=f32)
    total = image[...].astype(f32) * diag
    for piece, source in zip(pieces, sources(lax.axis_index("worker"))):
        block = image[pl.ds(pl.multiple_of(source * PART, PART), PART), :]
        total = total + jnp.dot(piece[...], block, preferred_element_type=f32)
    out[...] = total.astype(bf16).reshape(NB, ROWS, PART)


def pack_grams(holder, grams, *outs):
    worker = lax.axis_index("worker")
    for out, to in zip(outgoing(outs), dests(worker)):
        for c in range(CAP):
            out[c] = grams[jnp.maximum(holder[to * CAP + c], 0)]


def update(holder, left, right, *refs):
    pieces, outs, held, sems, out_sems = incoming(refs[:NW]), refs[NW : NW + 2], *refs[NW + 2 :]
    worker = lax.axis_index("worker")
    into = [
        [pltpu.make_async_copy(far.at[c], held.at[n, c], sems.at[n, c]) for c in range(CAP)]
        for n, far in enumerate((left, right))
    ]
    back = [
        [pltpu.make_async_copy(held.at[n, c], far.at[c], out_sems.at[n, c]) for c in range(CAP)]
        for n, far in enumerate(outs)
    ]
    for copies in into:
        for copy in copies:
            copy.start()
    for n in range(2):
        for c in range(CAP):
            into[n][c].wait()

            @pl.when(holder[worker * CAP + c] >= 0)
            def _():
                for piece, source in zip(pieces, sources(worker)):
                    cols = pl.ds(pl.multiple_of(source * PART, PART), PART)
                    gram = piece[c, n * ROWS : (n + 1) * ROWS, :].astype(f32)
                    held[n, c, :, cols] = (
                        decay_rate * held[n, c, :, cols] + (1.0 - decay_rate) * gram
                    )

            back[n][c].start()
    for copies in back:
        for copy in copies:
            copy.wait()


def assemble(*refs):
    pieces, out, sems = refs[:NW], refs[NW], refs[NW + 1]
    copies = []
    for j, source in enumerate(sources(lax.axis_index("worker"))):
        cols = pl.ds(pl.multiple_of(source * PART, PART), PART)
        copies.append(pltpu.make_async_copy(pieces[j], out.at[:, :, cols], sems.at[j]))
    for copy in copies:
        copy.start()
    for copy in copies:
        copy.wait()


def over_shard(value):
    return lax.all_to_all(value, "shard", 0, 0, tiled=True)


def body(grads, owners, left, right, left_root, right_root):
    tile = shape((NB, ROWS, PART))
    with jax.named_scope("roots"):
        *packed, mine, holder = call(
            pack_roots,
            [shape((2 * CAP * ROWS + HALF, PART))] * NW + [tile, shape((NW * CAP,), jnp.int32)],
            (owners[:, 0], left_root[0], right_root[0], grads),
            [SMEM, HBM, HBM, HBM],
            [VMEM] * (NW + 1) + [SMEM],
            [
                pltpu.VMEM((CAP, ROWS, BS), f32),
                pltpu.VMEM((CAP, ROWS, BS), f32),
                pltpu.SMEM((NW,), jnp.int32),
                pltpu.SemaphoreType.DMA((2, CAP)),
                pltpu.SemaphoreType.DMA((NB // 4,)),
            ],
            vmem=61,
        )
        mine, packed = lax.optimization_barrier((over_shard(mine), exchange(packed)))
    with jax.named_scope("gradients"):
        columns = gather(mine.reshape(BS, PART))
    with jax.named_scope("roots"):
        roots = call(
            pick_roots,
            shape((NB, 2 * ROWS + HALF, PART)),
            (holder, *packed),
            [SMEM] + [VMEM] * NW,
            vmem=61,
        )
        roots = over_shard(roots)
        root_l = gather(roots[:, :ROWS].reshape(BS, PART))
    with jax.named_scope("grams"):
        grams, image = call(
            make_grams,
            [shape((NB, 2 * ROWS, PART)), shape((BS, PART))],
            (roots, *columns),
            flops=6 * BS * BS * PART,
        )
        grams, root_l = lax.optimization_barrier((over_shard(grams), root_l))
        packed = call(
            pack_grams,
            [shape((CAP, 2 * ROWS, PART))] * 2 + [shape((2, CAP, 2 * ROWS, PART))] * 3,
            (holder, grams),
            [SMEM, VMEM],
            vmem=61,
        )
    with jax.named_scope("precondition"):
        result = call(
            make_result,
            tile,
            (roots, image, *root_l),
            flops=2 * BS * BS * PART,
        )
        own, given, *pairs = packed
        pairs = [send(pair, k, 0) for k, pair in enumerate(pairs, 1)]
        result, pairs, given = lax.optimization_barrier((over_shard(result), pairs, given))
        packed = [own, send(given, 0, 1)]
        for pair in pairs:
            packed += [pair, send(pair, 0, 1)]
    with jax.named_scope("factors"):
        factor = shape((CAP, ROWS, BS), f32)
        new_left, new_right = call(
            update,
            [factor, factor],
            (holder, left[0], right[0], *packed),
            [SMEM, HBM, HBM] + [VMEM] * NW,
            [HBM, HBM],
            [
                pltpu.VMEM((2, CAP, ROWS, BS), f32),
                pltpu.SemaphoreType.DMA((2, CAP)),
                pltpu.SemaphoreType.DMA((2, CAP)),
            ],
            nbytes=20 << 20,
            vmem=61,
        )
        own, new_left = lax.optimization_barrier((result, new_left))
    with jax.named_scope("precondition"):
        precond = call(
            assemble,
            shape((NB, ROWS, BS)),
            tuple(gather(result, own)),
            [VMEM] * NW,
            HBM,
            [pltpu.SemaphoreType.DMA((NW,))],
            nbytes=4 << 20,
        )
    return new_left[None], new_right[None], precond


def solution(mesh):
    factor = P("worker", None, "shard", None)
    return jax.shard_map(
        body,
        mesh=mesh,
        in_specs=(P(None, "shard", None), P(), factor, factor, factor, factor),
        out_specs=(factor, factor, P(None, "shard", None)),
        check_vma=False,
    )
```
